32 devices in a mesh: dp: 8 (over y, x, core), neg: 4 (over z).
Axes of the slice: x: 2, y: 2, z: 4, core: 2. Of those that a mesh axis runs over, the one named last changes fastest.
Arguments:
- queries: bfloat16 [4096, 4096], P('dp'), may hold values from -144 to 144, as said below
- passages: bfloat16 [8192, 4096], P(('dp', 'neg')), may hold values from -6 to 6
- list_owner: int32 [4, 1024, 1], P('neg', 'dp'), may hold values from 0 to 31; in each aligned block of 128 rows (0 to 127, 128 to 255, ..., all dimensions but the last counted through in order) at most 8 rows name the same one
- list_row: int32 [4, 1024], P('neg', 'dp'), may hold values from 0 to 255
- positive: int32 [4096], P('dp'), may hold values from 0 to 4095
- row_weight: float32 [4096], P('dp'), may hold values from 8 to 32
Outputs:
- query_grad: bfloat16 [4096, 4096], P('dp', 'neg')
- passage_grad: float32 [8192, 4096], P(('dp', 'neg'))
The draws below stay inside these ranges and needn't reach their ends.
Inputs may be any that keep to these rules, and one draw needn't show every extreme that they name: `queries`: queries are embedding activations. `list_owner`: among the 128 entries of one device no owner appears more than 8 times, and in every draw some device names some owner exactly 8 times.
All inputs are finite; a program needn't handle non-finite values.
Results may differ from the reference program's by a relative error of at most 0.015.
Values may be sent and summed in bfloat16 or wider, within the bound.
No kernel may reach another device: no remote copies, remote signals or barrier semaphores. Data moves between devices by JAX's collectives and lax.ppermute only.
A program may use at most 192 MiB of HBM per device.

```python
import math
import jax
import jax.numpy as jnp
import numpy as np
from jax import lax

D = 4096
Q_DEV = 512
LIST_DEV = 128
PASS_DEV = 256
CAP = 8
QUERIES = 4096
PASSAGES = 8192
BLOCK = 1024
COLS = 4096
N_DP = 8
N_NEG = 4
DEVICES = 32


def draw_queries(key, part):
    key = jax.random.fold_in(key, 11)
    base = jnp.clip(jax.random.normal(key, (QUERIES, D), jnp.float32), -6.0, 6.0)
    return base.astype(jnp.bfloat16)


def place_ends(result, rng, smallest, top_value):
    longest = result.shape.index(max(result.shape))
    spots = []
    for shift in (0, 1):
        where = [jax.random.randint(jax.random.fold_in(rng, axis), (), 0, length) for axis, length in enumerate(result.shape)]
        where[longest] = (where[longest] + shift) % result.shape[longest]
        spots.append(tuple(where))
    return result.at[spots[0]].set(smallest).at[spots[1]].set(top_value)


def shard_levels(key, extent, split, smallest, top_value):
    def one(position, blocks):
        heights = jax.random.uniform(jax.random.fold_in(jax.random.fold_in(key, 6), position), (blocks,), jnp.float32, smallest / len(split), top_value / len(split))
        return jnp.repeat(jnp.exp(heights), extent[position] // blocks).reshape((-1,) + (1,) * (len(extent) - position - 1))

    gain = one(*split[0])
    for cut in split[1:]:
        gain = gain * one(*cut)
    return gain


def rank_table(count, slope):
    loads = [(1 << 20) // math.isqrt(grade ** slope) + 1 for grade in range(1, count + 1)]
    width = 1 + sum(loads) // (1 << 30)
    return np.cumsum(np.array([max(1, weight // width) for weight in loads]))


def skewed_ids(rng, dims, number_of, skew):
    table = rank_table(number_of, skew)
    ticket = jax.random.randint(jax.random.fold_in(rng, 1), dims, 0, int(table[number_of - 1]))
    grade = jnp.searchsorted(jnp.asarray(table, jnp.int32), ticket, side="right")
    return jax.random.permutation(jax.random.fold_in(rng, 2), number_of)[grade].astype(jnp.int32)


def deal_out(rng, own, number, rows, count, top, limit, slope):
    sequence = jax.random.permutation(rng, count)
    packed, ordinary = shares(count, rows * top, limit, slope, True), shares(count, rows * top, limit, slope, False)
    places = jnp.arange(count)

    def named(lengths, turn):
        used = int((lengths > 0).sum())
        fixed = max(1, used // 4)
        passed = fixed + (places - fixed + turn * (used - fixed)) % max(1, count - fixed)
        return jnp.zeros((count,), jnp.int32).at[sequence[jnp.where(places < fixed, places, passed)]].set(jnp.asarray(lengths, jnp.int32))

    lengths = jnp.where(number % 4 == 0, named(packed, number // 4), named(ordinary, number - number // 4 - 1))
    mixed = jax.random.permutation(jax.random.fold_in(own, 3), count)
    source_of, sink = mixed[0:count // 2 * 2:2], mixed[1:count // 2 * 2:2]
    room = jnp.minimum(lengths[source_of] - 1, limit - lengths[sink]) // 2
    room = jnp.where((source_of == sequence[0]) | (sink == sequence[0]) | (lengths[sink] == 0), 0, jnp.maximum(room, 0))
    passed = jax.random.randint(jax.random.fold_in(own, 4), (count // 2,), 0, 1 << 20) % (room + 1)
    lengths = lengths.at[source_of].add(-passed).at[sink].add(passed)
    members = jnp.searchsorted(jnp.cumsum(lengths), jnp.arange(rows * top), side="right").astype(jnp.int32)
    grid = members.reshape(top, rows).T
    grid = grid[jax.random.permutation(jax.random.fold_in(own, 1), rows)]
    turn = jax.random.randint(jax.random.fold_in(own, 2), (rows, 1), 0, top)
    return jnp.take_along_axis(grid, (jnp.arange(top)[None, :] + turn) % top, axis=1)


def shares(count, total, most, skew, full):
    loads = [(1 << 20) // math.isqrt(grade ** skew) + 1 for grade in range(1, count + 1)]
    largest = most if full else min(most, max(-(-total // count), total * loads[0] // sum(loads)))
    least = 1 if total - largest >= count - 1 else 0
    counts, spare = [largest] + [least] * (count - 1), total - largest - least * (count - 1)
    while spare > 0:
        movable = [i for i in range(1, count) if counts[i] < largest] or [i for i in range(1, count) if counts[i] < most]
        whole, left = sum([loads[i] for i in movable]), spare
        for i in movable:
            more = min(most - counts[i], max(1, left * loads[i] // whole), spare)
            counts[i] = counts[i] + more
            spare = spare - more
    return np.array(counts)


def gaussian(stream_key, shape, deviation, limit, cuts=(), kind=jnp.bfloat16):
    result = jax.random.normal(stream_key, shape, jnp.float32) * deviation
    if len(cuts) > 0:
        result = shard_levels(stream_key, shape, cuts, -0.22, 0.18) * result
    return jnp.clip(result, min=-limit, max=limit).astype(kind)


def setup_inputs(seed: int = 0) -> dict:
    key_of = jax.random.split(jax.random.key(seed), 7)
    queries = draw_queries(jax.random.fold_in(key_of[6], 71), 0)
    passages = gaussian(key_of[1], (PASSAGES, D), 1.0, 6.0, ((0, 32),))
    list_owner_keys = jax.random.split(jax.random.fold_in(key_of[2], 1), N_NEG * BLOCK // LIST_DEV)
    list_owner_turns = jax.random.permutation(jax.random.fold_in(key_of[2], 3), N_NEG * BLOCK // LIST_DEV)
    list_owner = jax.vmap(lambda own, number: deal_out(jax.random.fold_in(key_of[2], 2), own, number, LIST_DEV, DEVICES, 1, CAP, 2))(list_owner_keys, list_owner_turns).reshape((N_NEG, BLOCK, 1))
    list_row = place_ends(skewed_ids(key_of[3], (N_NEG, BLOCK), PASS_DEV, 2), jax.random.fold_in(key_of[3], 3), 0, PASS_DEV - 1).astype(jnp.int32)
    positive = place_ends(jax.random.randint(key_of[4], (QUERIES,), 0, COLS), jax.random.fold_in(key_of[4], 1), 0, COLS - 1).astype(jnp.int32)
    row_weight = jnp.clip(jnp.exp(math.log(32.0) - 1.3862944 * jax.random.uniform(key_of[5], (QUERIES,), jnp.float32) ** shard_levels(key_of[5], (QUERIES,), ((0, 8),), -0.2, 0.2)), 8.0, 32.0)
    return dict(queries=queries, passages=passages, list_owner=list_owner, list_row=list_row, positive=positive, row_weight=row_weight)


def reference(queries, passages, list_owner, list_row, positive, row_weight):
    passage_ids = (list_owner[..., 0] * PASS_DEV + list_row).reshape(-1).astype(jnp.int32)
    columns = passages[passage_ids]
    logit_scale = 3.0 / math.sqrt(D)
    query_blocks = queries.reshape(N_DP, Q_DEV, D)
    pos_blocks = positive.reshape(N_DP, Q_DEV)
    weight_blocks = row_weight.reshape(N_DP, Q_DEV)
    col_index = jnp.arange(COLS, dtype=jnp.int32)

    def per_shard(carry, inputs):
        query_rows, pos_rows, weight_rows = inputs
        logits = jnp.dot(query_rows, columns.T, preferred_element_type=jnp.float32) * logit_scale
        row_max = lax.optimization_barrier(jnp.max(logits, axis=1, keepdims=True))
        expo = jnp.exp(logits - row_max)
        row_total = lax.optimization_barrier(jnp.sum(expo, axis=1, keepdims=True))
        target = (col_index[None, :] == pos_rows[:, None]).astype(jnp.float32)
        logit_grad = (weight_rows[:, None] * logit_scale * (expo / row_total - target)).astype(jnp.bfloat16)
        query_sum = jnp.zeros((Q_DEV, D), jnp.float32)
        for block_idx in range(N_NEG):
            lower = block_idx * BLOCK
            partial_value = jnp.dot(logit_grad[:, lower:lower + BLOCK], columns[lower:lower + BLOCK], preferred_element_type=jnp.float32)
            query_sum = query_sum + lax.optimization_barrier(partial_value.astype(jnp.bfloat16)).astype(jnp.float32)
        term = lax.dot_general(logit_grad, query_rows, (((0,), (0,)), ((), ())), preferred_element_type=jnp.float32)
        term = lax.optimization_barrier(term.astype(jnp.bfloat16)).astype(jnp.float32)
        return (carry + term, query_sum.astype(jnp.bfloat16))
    column_grad, query_grad = lax.scan(per_shard, jnp.zeros((COLS, D), jnp.float32), (query_blocks, pos_blocks, weight_blocks))
    passage_grad = jnp.zeros((PASSAGES, D), jnp.float32).at[passage_ids].add(column_grad)
    return (query_grad.reshape(QUERIES, D), passage_grad)
```

```python
import math

import jax
import jax.numpy as jnp
from jax import lax
from jax.sharding import PartitionSpec as P

F32 = jnp.float32
BF16 = jnp.bfloat16


def one_hot(index, size):
    return (index[:, None] == jnp.arange(size, dtype=jnp.int32)[None, :]).astype(BF16)


def dot_f32(a, b, dims):
    return lax.dot_general(a, b, (dims, ((), ())), preferred_element_type=F32)


def once(ready, value):
    corner = ready[(0,) * ready.ndim]
    return jnp.where(corner == corner, value, jnp.zeros_like(value))


def add_bf16(a, b):
    return (a.astype(F32) + b.astype(F32)).astype(BF16)


def shift_gather(value, axis, size):
    got = [value]
    for hop in range(1, size):
        got.append(lax.ppermute(value, axis, [(j, (j + hop) % size) for j in range(size)]))
    return got


def exchange(parts, axis):
    return lax.all_to_all(parts, axis, split_axis=0, concat_axis=0, tiled=True)


def swap(value, bit):
    return lax.ppermute(value, "dp", [(d, d ^ bit) for d in range(8)])


def rank_rows(counts):
    order = jnp.arange(counts.shape[1], dtype=jnp.int32)
    upto = (order[:, None] <= order[None, :]).astype(BF16)
    ends = dot_f32((counts > 0).astype(BF16), upto, ((1,), (0,))).astype(jnp.int32)
    return ends - 1, jnp.max(ends)


def pick_rows(room, counts, rank, mine):
    own_counts = lax.dynamic_index_in_dim(counts, mine, axis=0, keepdims=False)
    own_rank = lax.dynamic_index_in_dim(rank, mine, axis=0, keepdims=False)
    slots = jnp.arange(room, dtype=jnp.int32)
    return ((own_rank[None, :] == slots[:, None]) & (own_counts[None, :] > 0)).astype(BF16)


def lift_of(times):
    return jnp.where(times > 0, jnp.log(jnp.maximum(times, 1.0)), -1e30)


def describe_slots(room, counts, rank, first_id):
    slots = jnp.arange(room, dtype=jnp.int32)
    order = jnp.arange(counts.shape[1], dtype=jnp.int32)
    chosen = (rank[:, None, :] == slots[None, :, None]) & (counts[:, None, :] > 0)
    times = jnp.sum(jnp.where(chosen, counts[:, None, :], 0.0), axis=2)
    names = first_id[:, None] + order[None, :] + 1
    column_id = jnp.sum(jnp.where(chosen, names[:, None, :], 0), axis=2) - 1
    return lift_of(times), column_id


def logits_of(queries, columns, lift):
    scale = 3.0 / math.sqrt(queries.shape[1])
    return dot_f32(columns, queries, ((1,), (1,))) * scale + lift[:, None]


def softmax_grads(logits, column_ids, pos_id, row_weight, width, n_neg):
    factor = row_weight * (3.0 / math.sqrt(width))
    local_max = jnp.max(logits[0], axis=0)
    for group in logits[1:]:
        local_max = jnp.maximum(local_max, jnp.max(group, axis=0))
    expos = [jnp.exp(group - local_max[None, :]) for group in logits]
    local_sum = sum(jnp.sum(group, axis=0) for group in expos)
    stats = shift_gather(jnp.stack([local_max, local_sum]), "neg", n_neg)
    row_max = stats[0][0]
    for other in stats[1:]:
        row_max = jnp.maximum(row_max, other[0])
    row_total = sum(other[1] * jnp.exp(other[0] - row_max) for other in stats)
    share = factor * jnp.exp(local_max - row_max) / row_total
    return [
        (
            expo * share[None, :]
            - jnp.where(column_id[:, None] == pos_id[None, :], factor[None, :], 0.0)
        ).astype(BF16)
        for expo, column_id in zip(expos, column_ids)
    ]


def gather_cube(rows):
    half = rows.shape[0] // 2
    over_x = swap(rows, 2)
    over_y = swap(rows, 4)
    far = [swap(over_x[:half], 4), swap(over_y[half:], 2)]
    return rows, over_x, over_y, far


def scatter_cube(total):
    room = total.shape[0] // 4
    half = room // 2
    mine, to_x, to_y, far = [total[t * room:(t + 1) * room] for t in range(4)]
    far_first = swap(far[:half], 4)
    far_last = swap(far[half:], 2)
    x_last = swap(to_x[half:], 2)
    y_first = swap(to_y[:half], 4)
    x_first = swap(add_bf16(to_x[:half], far_first), 2)
    y_last = swap(add_bf16(to_y[half:], far_last), 4)
    from_x = jnp.concatenate([x_first, x_last])
    from_y = jnp.concatenate([y_first, y_last])
    return (mine.astype(F32) + from_x.astype(F32) + from_y.astype(F32)).astype(BF16)


def gradients_cube(room, queries, passages, counts, pos_id, row_weight, n_neg):
    pass_rows, width = passages.shape
    i_dp = lax.axis_index("dp")
    i_neg = lax.axis_index("neg")
    rank, _ = rank_rows(counts)
    pick = pick_rows(room, counts, rank, i_dp * n_neg + i_neg)
    rows = dot_f32(pick, passages, ((1,), (0,))).astype(BF16)
    rows = lax.optimization_barrier(rows)
    rows, over_x, over_y, far = gather_cube(rows)
    over_core = swap(rows, 1)

    turn = jnp.arange(8, dtype=jnp.int32)
    owners = (i_dp ^ (turn % 4 * 2 + turn // 4)) * n_neg + i_neg
    lift, slot_id = describe_slots(room, counts[owners], rank[owners], owners * pass_rows)

    groups, logits, column_ids = [], [], []

    def take(blocks, first, stop, step):
        groups.append(jnp.concatenate(blocks))
        logits.append(logits_of(queries, groups[-1], lift[first:stop:step].reshape(-1)))
        column_ids.append(slot_id[first:stop:step].reshape(-1))

    take([rows, over_core], 0, 5, 4)
    take([over_x, over_y], 1, 3, 1)
    take([swap(over_x, 1), swap(over_y, 1)], 5, 7, 1)
    far = once(logits[-1], jnp.concatenate(far))
    take([far, swap(far, 1)], 3, 8, 4)
    columns = jnp.concatenate(groups)
    grads = softmax_grads(logits, column_ids, pos_id, row_weight, width, n_neg)
    logit_grad = lax.optimization_barrier(jnp.concatenate(grads))
    query_part = dot_f32(logit_grad, columns, ((0,), (0,))).astype(BF16)
    query_grad = lax.psum_scatter(query_part, "neg", scatter_dimension=1, tiled=True)

    def grad_rows(*places):
        return jnp.concatenate([logit_grad[begin * room:stop * room] for begin, stop in places])

    across = dot_f32(grad_rows((1, 2), (4, 6), (7, 8)), queries, ((1,), (0,))).astype(BF16)
    near = dot_f32(grad_rows((0, 1), (2, 4), (6, 7)), queries, ((1,), (0,))).astype(BF16)
    column_grad = scatter_cube(add_bf16(near, swap(across, 1)))
    return query_grad, dot_f32(pick, column_grad, ((0,), (0,)))


def gradients_plain(room, queries, passages, counts, pos_id, row_weight, n_dp, n_neg):
    pass_rows, width = passages.shape
    rank, _ = rank_rows(counts)
    i_dp = lax.axis_index("dp")
    i_neg = lax.axis_index("neg")
    pick = pick_rows(room, counts, rank, i_dp * n_neg + i_neg)
    rows = dot_f32(pick, passages, ((1,), (0,))).astype(BF16)
    columns = exchange(jnp.broadcast_to(rows, (n_dp, room, width)), "dp")
    columns = columns.reshape(n_dp * room, width)
    owners = jnp.arange(n_dp, dtype=jnp.int32) * n_neg + i_neg
    lift, column_id = describe_slots(room, counts[owners], rank[owners], owners * pass_rows)
    logits = logits_of(queries, columns, lift.reshape(-1))
    (logit_grad,) = softmax_grads(
        [logits], [column_id.reshape(-1)], pos_id, row_weight, width, n_neg
    )
    query_part = dot_f32(logit_grad, columns, ((0,), (0,))).astype(BF16)
    query_part = query_part.reshape(query_part.shape[0], n_neg, -1).swapaxes(0, 1)
    query_grad = jnp.sum(exchange(query_part, "neg").astype(F32), axis=0).astype(BF16)
    column_part = dot_f32(logit_grad, queries, ((1,), (0,))).astype(BF16)
    column_part = column_part.reshape(n_dp, room, width)
    column_grad = jnp.sum(exchange(column_part, "dp").astype(F32), axis=0).astype(BF16)
    return query_grad, dot_f32(pick, column_grad, ((0,), (0,)))


def body(n_dp, n_neg, queries, passages, list_owner, list_row, positive, row_weight):
    devices = n_dp * n_neg
    pass_rows = passages.shape[0]
    list_len = list_row.shape[1]
    packed = list_owner.reshape(-1) * pass_rows + list_row.reshape(-1)
    ids = lax.all_to_all(
        jnp.broadcast_to(packed, (devices, list_len)),
        ("neg", "dp"),
        split_axis=0,
        concat_axis=0,
        tiled=True,
    ).reshape(-1)
    owner_of = ids // pass_rows
    row_of = ids % pass_rows
    counts = dot_f32(one_hot(owner_of, devices), one_hot(row_of, pass_rows), ((0,), (0,)))
    high = one_hot(positive // list_len, devices)
    low = one_hot(positive % list_len, list_len).astype(F32)
    owner_table = owner_of.reshape(-1, list_len).astype(BF16)
    row_table = row_of.reshape(-1, list_len).astype(BF16)
    pos_owner = jnp.sum(dot_f32(high, owner_table, ((1,), (0,))) * low, axis=1)
    pos_row = jnp.sum(dot_f32(high, row_table, ((1,), (0,))) * low, axis=1)
    pos_id = pos_owner.astype(jnp.int32) * pass_rows + pos_row.astype(jnp.int32)

    def plain(room):
        return gradients_plain(
            room, queries, passages, counts, pos_id, row_weight, n_dp, n_neg
        )

    _, longest = rank_rows(counts)
    if n_dp == 8:
        grads = gradients_cube(list_len, queries, passages, counts, pos_id, row_weight, n_neg)
    else:
        grads = plain(list_len)
    _, query_grad, passage_grad = lax.while_loop(
        lambda state: state[0],
        lambda state: (jnp.zeros((), jnp.bool_), *plain(pass_rows)),
        (longest > list_len, *grads),
    )
    return query_grad, passage_grad


def solution(mesh):
    n_dp, n_neg = mesh.shape["dp"], mesh.shape["neg"]
    in_specs = (
        P("dp", None),
        P(("dp", "neg"), None),
        P("neg", "dp", None),
        P("neg", "dp"),
        P("dp"),
        P("dp"),
    )
    out_specs = (P("dp", "neg"), P(("dp", "neg"), None))

    def run(*args):
        return body(n_dp, n_neg, *args)

    return jax.shard_map(run, mesh=mesh, in_specs=in_specs, out_specs=out_specs, check_vma=False)
```

```python
import math

import jax
import jax.numpy as jnp
from jax import lax
from jax.sharding import PartitionSpec as P

F32 = jnp.float32
BF16 = jnp.bfloat16


def one_hot(index, size):
    return (index[:, None] == jnp.arange(size, dtype=jnp.int32)[None, :]).astype(BF16)


def dot_f32(a, b, dims):
    return lax.dot_general(a, b, (dims, ((), ())), preferred_element_type=F32)


def once(ready, value):
    corner = ready[(0,) * ready.ndim]
    return jnp.where(corner == corner, value, jnp.zeros_like(value))


def add_bf16(a, b):
    return (a.astype(F32) + b.astype(F32)).astype(BF16)


def half_of(room):
    return (room // 2 + 15) // 16 * 16


def shift_gather(value, axis, size):
    got = [value]
    for hop in range(1, size):
        got.append(lax.ppermute(value, axis, [(j, (j + hop) % size) for j in range(size)]))
    return got


def exchange(parts, axis):
    return lax.all_to_all(parts, axis, split_axis=0, concat_axis=0, tiled=True)


def swap(value, bit):
    return lax.ppermute(value, "dp", [(d, d ^ bit) for d in range(8)])


def rank_rows(counts):
    order = jnp.arange(counts.shape[1], dtype=jnp.int32)
    upto = (order[:, None] <= order[None, :]).astype(BF16)
    ends = dot_f32((counts > 0).astype(BF16), upto, ((1,), (0,))).astype(jnp.int32)
    return ends - 1, jnp.max(ends)


def pick_rows(room, counts, rank, mine):
    own_counts = lax.dynamic_index_in_dim(counts, mine, axis=0, keepdims=False)
    own_rank = lax.dynamic_index_in_dim(rank, mine, axis=0, keepdims=False)
    slots = jnp.arange(room, dtype=jnp.int32)
    return ((own_rank[None, :] == slots[:, None]) & (own_counts[None, :] > 0)).astype(BF16)


def lift_of(times):
    return jnp.where(times > 0, jnp.log(jnp.maximum(times, 1.0)), -1e30)


def describe_slots(room, counts, rank, first_id):
    slots = jnp.arange(room, dtype=jnp.int32)
    order = jnp.arange(counts.shape[1], dtype=jnp.int32)
    chosen = (rank[:, None, :] == slots[None, :, None]) & (counts[:, None, :] > 0)
    times = jnp.sum(jnp.where(chosen, counts[:, None, :], 0.0), axis=2)
    names = first_id[:, None] + order[None, :] + 1
    column_id = jnp.sum(jnp.where(chosen, names[:, None, :], 0), axis=2) - 1
    return lift_of(times), column_id


def logits_of(queries, columns, lift):
    scale = 3.0 / math.sqrt(queries.shape[1])
    return dot_f32(columns, queries, ((1,), (1,))) * scale + lift[:, None]


def softmax_grads(logits, column_ids, pos_id, row_weight, width, n_neg):
    factor = row_weight * (3.0 / math.sqrt(width))
    local_max = jnp.max(logits[0], axis=0)
    for group in logits[1:]:
        local_max = jnp.maximum(local_max, jnp.max(group, axis=0))
    expos = [jnp.exp(group - local_max[None, :]) for group in logits]
    local_sum = sum(jnp.sum(group, axis=0) for group in expos)
    stats = shift_gather(jnp.stack([local_max, local_sum]), "neg", n_neg)
    row_max = stats[0][0]
    for other in stats[1:]:
        row_max = jnp.maximum(row_max, other[0])
    row_total = sum(other[1] * jnp.exp(other[0] - row_max) for other in stats)
    share = factor * jnp.exp(local_max - row_max) / row_total
    return [
        (
            expo * share[None, :]
            - jnp.where(column_id[:, None] == pos_id[None, :], factor[None, :], 0.0)
        ).astype(BF16)
        for expo, column_id in zip(expos, column_ids)
    ]


def scatter_cube(total):
    room = total.shape[0] // 4
    half = half_of(room)
    mine, to_x, to_y, far = [total[t * room:(t + 1) * room] for t in range(4)]
    far_first = swap(far[:half], 4)
    far_last = swap(far[half:], 2)
    x_last = swap(to_x[half:], 2)
    y_first = swap(to_y[:half], 4)
    x_first = swap(add_bf16(to_x[:half], far_first), 2)
    y_last = swap(add_bf16(to_y[half:], far_last), 4)
    from_x = jnp.concatenate([x_first, x_last])
    from_y = jnp.concatenate([y_first, y_last])
    return (mine.astype(F32) + from_x.astype(F32) + from_y.astype(F32)).astype(BF16)


def gradients_cube(room, queries, passages, counts, pos_id, row_weight, n_neg):
    pass_rows, width = passages.shape
    i_dp = lax.axis_index("dp")
    i_neg = lax.axis_index("neg")
    rank, _ = rank_rows(counts)
    pick = pick_rows(room, counts, rank, i_dp * n_neg + i_neg)
    rows = dot_f32(pick, passages, ((1,), (0,))).astype(BF16)
    rows = lax.optimization_barrier(rows)
    over_x = swap(rows, 2)
    over_y = swap(rows, 4)
    over_core = swap(rows, 1)

    turn = jnp.arange(8, dtype=jnp.int32)
    owners = (i_dp ^ (turn % 4 * 2 + turn // 4)) * n_neg + i_neg
    lift, slot_id = describe_slots(room, counts[owners], rank[owners], owners * pass_rows)

    groups, logits, column_ids = [], [], []

    def take(blocks, first, stop, step):
        group_lift = lift[first:stop:step].reshape(-1)
        if len(logits) == 2:
            group_lift = once(logits[0], group_lift)
        groups.append(jnp.concatenate(blocks))
        logits.append(logits_of(queries, groups[-1], group_lift))
        column_ids.append(slot_id[first:stop:step].reshape(-1))

    take([rows, over_core], 0, 5, 4)
    half = half_of(room)
    far = [swap(over_x[:half], 4), swap(over_y[half:], 2)]
    take([over_x, over_y], 1, 3, 1)
    take([swap(over_x, 1), swap(over_y, 1)], 5, 7, 1)
    far = once(logits[-1], jnp.concatenate(far))
    take([far, swap(far, 1)], 3, 8, 4)
    columns = jnp.concatenate(groups)
    grads = softmax_grads(logits, column_ids, pos_id, row_weight, width, n_neg)
    logit_grad = lax.optimization_barrier(jnp.concatenate(grads))
    query_part = dot_f32(logit_grad, columns, ((0,), (0,))).astype(BF16)
    query_grad = lax.psum_scatter(query_part, "neg", scatter_dimension=1, tiled=True)

    def grad_rows(*places):
        return jnp.concatenate([logit_grad[begin * room:stop * room] for begin, stop in places])

    across = dot_f32(grad_rows((1, 2), (4, 6), (7, 8)), queries, ((1,), (0,))).astype(BF16)
    near = dot_f32(grad_rows((0, 1), (2, 4), (6, 7)), queries, ((1,), (0,))).astype(BF16)
    column_grad = scatter_cube(add_bf16(near, swap(across, 1)))
    return query_grad, dot_f32(pick, column_grad, ((0,), (0,)))


def gradients_plain(room, queries, passages, counts, pos_id, row_weight, n_dp, n_neg):
    pass_rows, width = passages.shape
    rank, _ = rank_rows(counts)
    i_dp = lax.axis_index("dp")
    i_neg = lax.axis_index("neg")
    pick = pick_rows(room, counts, rank, i_dp * n_neg + i_neg)
    rows = dot_f32(pick, passages, ((1,), (0,))).astype(BF16)
    columns = exchange(jnp.broadcast_to(rows, (n_dp, room, width)), "dp")
    columns = columns.reshape(n_dp * room, width)
    owners = jnp.arange(n_dp, dtype=jnp.int32) * n_neg + i_neg
    lift, column_id = describe_slots(room, counts[owners], rank[owners], owners * pass_rows)
    logits = logits_of(queries, columns, lift.reshape(-1))
    (logit_grad,) = softmax_grads(
        [logits], [column_id.reshape(-1)], pos_id, row_weight, width, n_neg
    )
    query_part = dot_f32(logit_grad, columns, ((0,), (0,))).astype(BF16)
    query_part = query_part.reshape(query_part.shape[0], n_neg, -1).swapaxes(0, 1)
    query_grad = jnp.sum(exchange(query_part, "neg").astype(F32), axis=0).astype(BF16)
    column_part = dot_f32(logit_grad, queries, ((1,), (0,))).astype(BF16)
    column_part = column_part.reshape(n_dp, room, width)
    column_grad = jnp.sum(exchange(column_part, "dp").astype(F32), axis=0).astype(BF16)
    return query_grad, dot_f32(pick, column_grad, ((0,), (0,)))


def body(n_dp, n_neg, queries, passages, list_owner, list_row, positive, row_weight):
    devices = n_dp * n_neg
    pass_rows = passages.shape[0]
    list_len = list_row.shape[1]
    packed = list_owner.reshape(-1) * pass_rows + list_row.reshape(-1)
    ids = lax.all_to_all(
        jnp.broadcast_to(packed, (devices, list_len)),
        ("neg", "dp"),
        split_axis=0,
        concat_axis=0,
        tiled=True,
    ).reshape(-1)
    owner_of = ids // pass_rows
    row_of = ids % pass_rows
    counts = dot_f32(one_hot(owner_of, devices), one_hot(row_of, pass_rows), ((0,), (0,)))
    high = one_hot(positive // list_len, devices)
    low = one_hot(positive % list_len, list_len).astype(F32)
    owner_table = owner_of.reshape(-1, list_len).astype(BF16)
    row_table = row_of.reshape(-1, list_len).astype(BF16)
    pos_owner = jnp.sum(dot_f32(high, owner_table, ((1,), (0,))) * low, axis=1)
    pos_row = jnp.sum(dot_f32(high, row_table, ((1,), (0,))) * low, axis=1)
    pos_id = pos_owner.astype(jnp.int32) * pass_rows + pos_row.astype(jnp.int32)

    def plain(room):
        return gradients_plain(
            room, queries, passages, counts, pos_id, row_weight, n_dp, n_neg
        )

    _, longest = rank_rows(counts)
    room = list_len
    if n_dp == 8:
        room = list_len - list_len // 8
        grads = gradients_cube(room, queries, passages, counts, pos_id, row_weight, n_neg)
    else:
        grads = plain(room)
    _, query_grad, passage_grad = lax.while_loop(
        lambda state: state[0],
        lambda state: (jnp.zeros((), jnp.bool_), *plain(pass_rows)),
        (longest > room, *grads),
    )
    return query_grad, passage_grad


def solution(mesh):
    n_dp, n_neg = mesh.shape["dp"], mesh.shape["neg"]
    in_specs = (
        P("dp", None),
        P(("dp", "neg"), None),
        P("neg", "dp", None),
        P("neg", "dp"),
        P("dp"),
        P("dp"),
    )
    out_specs = (P("dp", "neg"), P(("dp", "neg"), None))

    def run(*args):
        return body(n_dp, n_neg, *args)

    return jax.shard_map(run, mesh=mesh, in_specs=in_specs, out_specs=out_specs, check_vma=False)
```

```python
import math

import jax
import jax.numpy as jnp
from jax import lax
from jax.sharding import PartitionSpec as P

F32 = jnp.float32
BF16 = jnp.bfloat16


def one_hot(index, size):
    return (index[:, None] == jnp.arange(size, dtype=jnp.int32)[None, :]).astype(BF16)


def dot_f32(a, b, dims):
    return lax.dot_general(a, b, (dims, ((), ())), preferred_element_type=F32)


def once(ready, value):
    corner = ready[(0,) * ready.ndim]
    return jnp.where(corner == corner, value, jnp.zeros_like(value))


def add_bf16(a, b):
    return (a.astype(F32) + b.astype(F32)).astype(BF16)


def shift_gather(value, axis, size):
    got = [value]
    for hop in range(1, size):
        got.append(lax.ppermute(value, axis, [(j, (j + hop) % size) for j in range(size)]))
    return got


def exchange(parts, axis):
    return lax.all_to_all(parts, axis, split_axis=0, concat_axis=0, tiled=True)


def swap(value, bit):
    return lax.ppermute(value, "dp", [(d, d ^ bit) for d in range(8)])


def rank_rows(counts):
    order = jnp.arange(counts.shape[1], dtype=jnp.int32)
    upto = (order[:, None] <= order[None, :]).astype(BF16)
    ends = dot_f32((counts > 0).astype(BF16), upto, ((1,), (0,))).astype(jnp.int32)
    return ends - 1, jnp.max(ends)


def pick_rows(room, counts, rank, mine):
    own_counts = lax.dynamic_index_in_dim(counts, mine, axis=0, keepdims=False)
    own_rank = lax.dynamic_index_in_dim(rank, mine, axis=0, keepdims=False)
    slots = jnp.arange(room, dtype=jnp.int32)
    return ((own_rank[None, :] == slots[:, None]) & (own_counts[None, :] > 0)).astype(BF16)


def lift_of(times):
    return jnp.where(times > 0, jnp.log(jnp.maximum(times, 1.0)), -1e30)


def describe_slots(room, counts, rank, first_id):
    slots = jnp.arange(room, dtype=jnp.int32)
    order = jnp.arange(counts.shape[1], dtype=jnp.int32)
    chosen = (rank[:, None, :] == slots[None, :, None]) & (counts[:, None, :] > 0)
    times = jnp.sum(jnp.where(chosen, counts[:, None, :], 0.0), axis=2)
    names = first_id[:, None] + order[None, :] + 1
    column_id = jnp.sum(jnp.where(chosen, names[:, None, :], 0), axis=2) - 1
    return lift_of(times), column_id


def logits_of(queries, columns, lift):
    scale = 3.0 / math.sqrt(queries.shape[1])
    return dot_f32(columns, queries, ((1,), (1,))) * scale + lift[:, None]


def softmax_grads(logits, column_ids, pos_id, row_weight, width, n_neg):
    factor = row_weight * (3.0 / math.sqrt(width))
    local_max = jnp.max(logits[0], axis=0)
    for group in logits[1:]:
        local_max = jnp.maximum(local_max, jnp.max(group, axis=0))
    expos = [jnp.exp(group - local_max[None, :]) for group in logits]
    local_sum = sum(jnp.sum(group, axis=0) for group in expos)
    stats = shift_gather(jnp.stack([local_max, local_sum]), "neg", n_neg)
    row_max = stats[0][0]
    for other in stats[1:]:
        row_max = jnp.maximum(row_max, other[0])
    row_total = sum(other[1] * jnp.exp(other[0] - row_max) for other in stats)
    share = factor * jnp.exp(local_max - row_max) / row_total
    return [
        (
            expo * share[None, :]
            - jnp.where(column_id[:, None] == pos_id[None, :], factor[None, :], 0.0)
        ).astype(BF16)
        for expo, column_id in zip(expos, column_ids)
    ]


def gather_cube(rows):
    half = rows.shape[0] // 2
    over_x = swap(rows, 2)
    over_y = swap(rows, 4)
    far = [swap(over_x[:half], 4), swap(over_y[half:], 2)]
    return rows, over_x, over_y, far


def scatter_cube(total):
    room = total.shape[0] // 4
    half = room // 2
    mine, to_x, to_y, far = [total[t * room:(t + 1) * room] for t in range(4)]
    far_first = swap(far[:half], 4)
    far_last = swap(far[half:], 2)
    x_last = swap(to_x[half:], 2)
    y_first = swap(to_y[:half], 4)
    x_first = swap(add_bf16(to_x[:half], far_first), 2)
    y_last = swap(add_bf16(to_y[half:], far_last), 4)
    from_x = jnp.concatenate([x_first, x_last])
    from_y = jnp.concatenate([y_first, y_last])
    return (mine.astype(F32) + from_x.astype(F32) + from_y.astype(F32)).astype(BF16)


def gradients_cube(room, queries, passages, counts, pos_id, row_weight, n_neg):
    pass_rows, width = passages.shape
    i_dp = lax.axis_index("dp")
    i_neg = lax.axis_index("neg")
    rank, _ = rank_rows(counts)
    pick = pick_rows(room, counts, rank, i_dp * n_neg + i_neg)
    rows = dot_f32(pick, passages, ((1,), (0,))).astype(BF16)
    rows = lax.optimization_barrier(rows)
    rows, over_x, over_y, far = gather_cube(rows)
    over_core = swap(rows, 1)

    turn = jnp.arange(8, dtype=jnp.int32)
    owners = (i_dp ^ (turn % 4 * 2 + turn // 4)) * n_neg + i_neg
    lift, slot_id = describe_slots(room, counts[owners], rank[owners], owners * pass_rows)

    groups, logits, column_ids = [], [], []

    def take(blocks, first, stop, step):
        group_lift = lift[first:stop:step].reshape(-1)
        if len(logits) == 2:
            group_lift = once(logits[0], group_lift)
        groups.append(jnp.concatenate(blocks))
        logits.append(logits_of(queries, groups[-1], group_lift))
        column_ids.append(slot_id[first:stop:step].reshape(-1))

    take([rows, over_core], 0, 5, 4)
    take([over_x, over_y], 1, 3, 1)
    take([swap(over_x, 1), swap(over_y, 1)], 5, 7, 1)
    far = once(logits[-1], jnp.concatenate(far))
    take([far, swap(far, 1)], 3, 8, 4)
    columns = jnp.concatenate(groups)
    grads = softmax_grads(logits, column_ids, pos_id, row_weight, width, n_neg)
    logit_grad = lax.optimization_barrier(jnp.concatenate(grads))
    query_part = dot_f32(logit_grad, columns, ((0,), (0,))).astype(BF16)
    query_grad = lax.psum_scatter(query_part, "neg", scatter_dimension=1, tiled=True)

    def grad_rows(*places):
        return jnp.concatenate([logit_grad[begin * room:stop * room] for begin, stop in places])

    across = dot_f32(grad_rows((1, 2), (4, 6), (7, 8)), queries, ((1,), (0,))).astype(BF16)
    near = dot_f32(grad_rows((0, 1), (2, 4), (6, 7)), queries, ((1,), (0,))).astype(BF16)
    column_grad = scatter_cube(add_bf16(near, swap(across, 1)))
    return query_grad, dot_f32(pick, column_grad, ((0,), (0,)))


def gradients_plain(room, queries, passages, counts, pos_id, row_weight, n_dp, n_neg):
    pass_rows, width = passages.shape
    rank, _ = rank_rows(counts)
    i_dp = lax.axis_index("dp")
    i_neg = lax.axis_index("neg")
    pick = pick_rows(room, counts, rank, i_dp * n_neg + i_neg)
    rows = dot_f32(pick, passages, ((1,), (0,))).astype(BF16)
    columns = exchange(jnp.broadcast_to(rows, (n_dp, room, width)), "dp")
    columns = columns.reshape(n_dp * room, width)
    owners = jnp.arange(n_dp, dtype=jnp.int32) * n_neg + i_neg
    lift, column_id = describe_slots(room, counts[owners], rank[owners], owners * pass_rows)
    logits = logits_of(queries, columns, lift.reshape(-1))
    (logit_grad,) = softmax_grads(
        [logits], [column_id.reshape(-1)], pos_id, row_weight, width, n_neg
    )
    query_part = dot_f32(logit_grad, columns, ((0,), (0,))).astype(BF16)
    query_part = query_part.reshape(query_part.shape[0], n_neg, -1).swapaxes(0, 1)
    query_grad = jnp.sum(exchange(query_part, "neg").astype(F32), axis=0).astype(BF16)
    column_part = dot_f32(logit_grad, queries, ((1,), (0,))).astype(BF16)
    column_part = column_part.reshape(n_dp, room, width)
    column_grad = jnp.sum(exchange(column_part, "dp").astype(F32), axis=0).astype(BF16)
    return query_grad, dot_f32(pick, column_grad, ((0,), (0,)))


def body(n_dp, n_neg, queries, passages, list_owner, list_row, positive, row_weight):
    devices = n_dp * n_neg
    pass_rows = passages.shape[0]
    list_len = list_row.shape[1]
    packed = list_owner.reshape(-1) * pass_rows + list_row.reshape(-1)
    ids = lax.all_to_all(
        jnp.broadcast_to(packed, (devices, list_len)),
        ("neg", "dp"),
        split_axis=0,
        concat_axis=0,
        tiled=True,
    ).reshape(-1)
    owner_of = ids // pass_rows
    row_of = ids % pass_rows
    counts = dot_f32(one_hot(owner_of, devices), one_hot(row_of, pass_rows), ((0,), (0,)))
    high = one_hot(positive // list_len, devices)
    low = one_hot(positive % list_len, list_len).astype(F32)
    owner_table = owner_of.reshape(-1, list_len).astype(BF16)
    row_table = row_of.reshape(-1, list_len).astype(BF16)
    pos_owner = jnp.sum(dot_f32(high, owner_table, ((1,), (0,))) * low, axis=1)
    pos_row = jnp.sum(dot_f32(high, row_table, ((1,), (0,))) * low, axis=1)
    pos_id = pos_owner.astype(jnp.int32) * pass_rows + pos_row.astype(jnp.int32)

    def plain(room):
        return gradients_plain(
            room, queries, passages, counts, pos_id, row_weight, n_dp, n_neg
        )

    _, longest = rank_rows(counts)
    if n_dp == 8:
        grads = gradients_cube(list_len, queries, passages, counts, pos_id, row_weight, n_neg)
    else:
        grads = plain(list_len)
    _, query_grad, passage_grad = lax.while_loop(
        lambda state: state[0],
        lambda state: (jnp.zeros((), jnp.bool_), *plain(pass_rows)),
        (longest > list_len, *grads),
    )
    return query_grad, passage_grad


def solution(mesh):
    n_dp, n_neg = mesh.shape["dp"], mesh.shape["neg"]
    in_specs = (
        P("dp", None),
        P(("dp", "neg"), None),
        P("neg", "dp", None),
        P("neg", "dp"),
        P("dp"),
        P("dp"),
    )
    out_specs = (P("dp", "neg"), P(("dp", "neg"), None))

    def run(*args):
        return body(n_dp, n_neg, *args)

    return jax.shard_map(run, mesh=mesh, in_specs=in_specs, out_specs=out_specs, check_vma=False)
```

```python
import math

import jax
import jax.numpy as jnp
from jax import lax
from jax.sharding import PartitionSpec as P

F32 = jnp.float32
BF16 = jnp.bfloat16


def one_hot(index, size):
    return (index[:, None] == jnp.arange(size, dtype=jnp.int32)[None, :]).astype(BF16)


def dot_f32(a, b, dims):
    return lax.dot_general(a, b, (dims, ((), ())), preferred_element_type=F32)


def shift_gather(value, axis, size):
    got = [value]
    for hop in range(1, size):
        got.append(lax.ppermute(value, axis, [(j, (j + hop) % size) for j in range(size)]))
    return got


def swap(value, bit, size):
    return lax.ppermute(value, "dp", [(d, d ^ bit) for d in range(size)])


def after(value, *earlier):
    return lax.optimization_barrier((value, earlier))[0]


def gather_cube(rows):
    half = rows.shape[0] // 2
    over_x = swap(rows, 2, 8)
    over_y = swap(rows, 4, 8)
    over_core = swap(rows, 1, 8)
    first = swap(over_x[:half], 4, 8)
    last = swap(over_y[half:], 2, 8)
    x_core = swap(over_x, 1, 8)
    y_core = swap(over_y, 1, 8)
    far = jnp.concatenate([first, last])
    far_core = swap(far, 1, 8)
    return [rows, over_x, over_y, far, over_core, x_core, y_core, far_core]


def cube_order(index):
    return index ^ jnp.array([0, 2, 4, 6, 1, 3, 5, 7], jnp.int32)


def add_bf16(a, b):
    return (a.astype(F32) + b.astype(F32)).astype(BF16)


def reduce_products(logit_grad, columns, queries, n_dp):
    query_part = dot_f32(logit_grad, columns, ((1,), (0,))).astype(BF16)
    query_grad = lax.psum_scatter(query_part, "neg", scatter_dimension=1, tiled=True)
    logit_grad = after(logit_grad, query_part)
    if n_dp != 8:
        column_part = dot_f32(logit_grad, queries, ((0,), (0,))).astype(BF16)
        column_grad = lax.psum_scatter(column_part, "dp", scatter_dimension=0, tiled=True)
        return query_grad, column_grad
    middle = logit_grad.shape[1] // 2
    room = middle // 4
    half = room // 2
    across = dot_f32(logit_grad[:, middle:], queries, ((0,), (0,))).astype(BF16)
    over_core = swap(across, 1, 8)
    near = dot_f32(after(logit_grad, across)[:, :middle], queries, ((0,), (0,))).astype(BF16)
    total = add_bf16(near, over_core)
    own, to_x, to_y, far = [total[t * room:(t + 1) * room] for t in range(4)]
    far_first = swap(far[:half], 4, 8)
    far_last = swap(far[half:], 2, 8)
    x_last = swap(to_x[half:], 2, 8)
    y_first = swap(to_y[:half], 4, 8)
    x_first = swap(add_bf16(to_x[:half], far_first), 2, 8)
    y_last = swap(add_bf16(to_y[half:], far_last), 4, 8)
    from_x = jnp.concatenate([x_first, x_last])
    from_y = jnp.concatenate([y_first, y_last])
    column_grad = (own.astype(F32) + from_x.astype(F32) + from_y.astype(F32)).astype(BF16)
    return query_grad, column_grad


def gradients(cube, room, queries, passages, counts, rank, pos_id, row_weight, n_dp, n_neg):
    pass_rows, width = passages.shape
    i_dp = lax.axis_index("dp")
    i_neg = lax.axis_index("neg")
    mine = i_dp * n_neg + i_neg
    slots = jnp.arange(room, dtype=jnp.int32)
    own_counts = lax.dynamic_index_in_dim(counts, mine, axis=0, keepdims=False)
    own_rank = lax.dynamic_index_in_dim(rank, mine, axis=0, keepdims=False)
    pick = (
        (own_rank[None, :] == slots[:, None]) & (own_counts[None, :] > 0)
    ).astype(BF16)
    own_rows = dot_f32(pick, passages, ((1,), (0,))).astype(BF16)
    own_rows = lax.optimization_barrier(own_rows)
    if cube:
        blocks = gather_cube(own_rows)
        arrivals = [[0, 4], [1, 2, 5, 6], [3, 7]]
    else:
        blocks = [lax.all_gather(own_rows, "dp", axis=0, tiled=True)]
        arrivals = [[0]]
    columns = jnp.concatenate(blocks)

    order = cube_order(i_dp) if cube else jnp.arange(n_dp, dtype=jnp.int32)
    owner_order = order * n_neg + i_neg
    plane_counts = counts[owner_order]
    plane_rank = rank[owner_order]
    chosen = (plane_rank[:, None, :] == slots[None, :, None]) & (plane_counts[:, None, :] > 0)
    times = jnp.sum(jnp.where(chosen, plane_counts[:, None, :], 0.0), axis=2).reshape(-1)
    names = owner_order[:, None] * pass_rows + jnp.arange(pass_rows, dtype=jnp.int32)[None, :] + 1
    column_id = jnp.sum(jnp.where(chosen, names[:, None, :], 0), axis=2).reshape(-1) - 1
    lift = jnp.where(times > 0, jnp.log(jnp.maximum(times, 1.0)), -1e30)
    target = pos_id[:, None] == column_id[None, :]

    scale = 3.0 / math.sqrt(width)
    factor = row_weight * scale
    lift = lift.reshape(len(blocks), -1)
    logits = [None] * len(blocks)
    for members in arrivals:
        group = jnp.concatenate([blocks[t] for t in members])
        lifts = jnp.concatenate([lift[t] for t in members])
        value = dot_f32(queries, group, ((1,), (1,))) * scale + lifts[None, :]
        for t, part in zip(members, jnp.split(value, len(members), axis=1)):
            logits[t] = part
    logits = jnp.concatenate(logits, axis=1)
    local_max = jnp.max(logits, axis=1)
    expo = jnp.exp(logits - local_max[:, None])
    local_sum = jnp.sum(expo, axis=1)
    stats = shift_gather(jnp.stack([local_max, local_sum]), "neg", n_neg)
    row_max = stats[0][0]
    for other in stats[1:]:
        row_max = jnp.maximum(row_max, other[0])
    row_total = sum(other[1] * jnp.exp(other[0] - row_max) for other in stats)
    share = factor * jnp.exp(local_max - row_max) / row_total
    logit_grad = (
        expo * share[:, None] - jnp.where(target, factor[:, None], 0.0)
    ).astype(BF16)
    logit_grad = lax.optimization_barrier(logit_grad)
    query_grad, column_grad = reduce_products(
        logit_grad, columns, queries, n_dp if cube else 0
    )
    passage_grad = dot_f32(pick, column_grad, ((0,), (0,)))
    return query_grad, passage_grad


def body(n_dp, n_neg, queries, passages, list_owner, list_row, positive, row_weight):
    devices = n_dp * n_neg
    pass_rows = passages.shape[0]
    list_len = list_row.shape[1]
    packed = list_owner.reshape(-1) * pass_rows + list_row.reshape(-1)
    ids = lax.all_to_all(
        jnp.broadcast_to(packed, (devices, list_len)),
        ("neg", "dp"),
        split_axis=0,
        concat_axis=0,
        tiled=True,
    ).reshape(-1)
    owner_of = ids // pass_rows
    row_of = ids % pass_rows
    counts = dot_f32(one_hot(owner_of, devices), one_hot(row_of, pass_rows), ((0,), (0,)))
    present = counts > 0
    order = jnp.arange(pass_rows, dtype=jnp.int32)
    upto = (order[:, None] <= order[None, :]).astype(BF16)
    ends = dot_f32(present.astype(BF16), upto, ((1,), (0,))).astype(jnp.int32)
    rank = ends - 1
    longest = jnp.max(ends)

    high = one_hot(positive // list_len, devices)
    low = one_hot(positive % list_len, list_len).astype(F32)
    owner_table = owner_of.reshape(-1, list_len).astype(BF16)
    row_table = row_of.reshape(-1, list_len).astype(BF16)
    pos_owner = jnp.sum(dot_f32(high, owner_table, ((1,), (0,))) * low, axis=1)
    pos_row = jnp.sum(dot_f32(high, row_table, ((1,), (0,))) * low, axis=1)
    pos_id = pos_owner.astype(jnp.int32) * pass_rows + pos_row.astype(jnp.int32)

    def run(cube, room):
        return lambda: gradients(
            cube, room, queries, passages, counts, rank, pos_id, row_weight, n_dp, n_neg
        )

    return lax.cond(longest <= list_len, run(n_dp == 8, list_len), run(False, pass_rows))


def solution(mesh):
    n_dp, n_neg = mesh.shape["dp"], mesh.shape["neg"]
    in_specs = (
        P("dp", None),
        P(("dp", "neg"), None),
        P("neg", "dp", None),
        P("neg", "dp"),
        P("dp"),
        P("dp"),
    )
    out_specs = (P("dp", "neg"), P(("dp", "neg"), None))

    def run(*args):
        return body(n_dp, n_neg, *args)

    return jax.shard_map(run, mesh=mesh, in_specs=in_specs, out_specs=out_specs, check_vma=False)
```
